512 devices in a mesh: batch: 16 (over y, x), centre: 32 (over z, core).
Axes of the slice: x: 4, y: 4, z: 16, core: 2. Of those that a mesh axis runs over, the one named last changes fastest.
Arguments:
- pool: float32 [4096, 1024], P('batch', 'centre'), may hold values from -4.5 to 4.5
- sample_index: int32 [2048], P('batch'), may hold values from 0 to 255
- targets: float32 [2048, 256], P('batch'), may hold values from -6 to 6
- centres: float32 [8192, 1024], P(('batch', 'centre')), may hold values from -4.5 to 4.5
- coeffs: float32 [8192, 256], P(('batch', 'centre')), may hold values from -6 to 6
- eigvecs: float32 [8192, 1024], P(('batch', 'centre')), may hold values from -0.1875 to 0.1875
- eigscale: float32 [1024], replicated, may hold values from 0.1 to 0.95
Outputs:
- new_coeffs: float32 [8192, 256], P(('batch', 'centre'))
The draws below stay inside these ranges and needn't reach their ends.
Inputs may be any that keep to these rules, and one draw needn't show every extreme that they name: `sample_index`: each batch row's sample lies in the block of 256 training samples held by its own batch group; the index counts within that block.
All inputs are finite; a program needn't handle non-finite values.
Results may differ from the reference program's by a relative error of at most 0.0003.
Values sent between devices are 32-bit elements; how exact they have to be, the bound alone decides.
No kernel may reach another device: no remote copies, remote signals or barrier semaphores. Data moves between devices by JAX's collectives and lax.ppermute only.
A program may use at most 64 MiB of HBM per device.

```python
import jax
import jax.numpy as jnp
from jax import lax

FEATURES = 1024
OUTPUTS = 256
EIGEN = 1024
ROWS_DEV = 128
SAMPLES_DEV = 256
ROWS = 2048
CENTRES = 8192
POOL = 4096
N_BATCH = 16


def plant(array, rng, least, high):
    dims = array.shape
    place = [jax.random.randint(jax.random.fold_in(rng, axis), (), 0, dims[axis]) for axis in range(len(dims))]
    array = array.at[tuple(place)].set(least)
    longest = dims.index(max(dims))
    place[longest] = (place[longest] + 1) % dims[longest]
    return array.at[tuple(place)].set(high)


def block_scale(own_key, extent, cuts, low, top_value):
    level, own = 1.0, jax.random.fold_in(own_key, 6)
    for axis_at, shards_of in cuts:
        draws = jnp.exp(jax.random.uniform(jax.random.fold_in(own, axis_at), (shards_of,), jnp.float32, low / len(cuts), top_value / len(cuts)))
        level = level * jnp.repeat(draws, extent[axis_at] // shards_of).reshape([-1 if axis == axis_at else 1 for axis in range(len(extent))])
    return level


def bell_draw(own_key, dims, width, limit, shards=(), held_as=jnp.bfloat16):
    gain = block_scale(own_key, dims, shards, -0.22, 0.18) if shards else 1.0
    values = jax.random.normal(own_key, dims, jnp.float32) * width * gain
    return jnp.minimum(jnp.maximum(values, -limit), limit).astype(held_as)


def setup_inputs(seed: int = 0) -> dict:
    key_of = jax.random.split(jax.random.key(seed), 8)
    return {
        "pool": bell_draw(key_of[0], (POOL, FEATURES), 0.75, 4.5, ((0, 16), (1, 32)), jnp.float32),
        "sample_index": plant(jax.random.randint(key_of[1], (ROWS,), 0, SAMPLES_DEV), jax.random.fold_in(key_of[1], 1), 0, SAMPLES_DEV - 1).astype(jnp.int32),
        "targets": bell_draw(key_of[2], (ROWS, OUTPUTS), 1.0, 6.0, ((0, 16),), jnp.float32),
        "centres": bell_draw(key_of[3], (CENTRES, FEATURES), 0.75, 4.5, ((0, 512),), jnp.float32),
        "coeffs": bell_draw(key_of[4], (CENTRES, OUTPUTS), 1.0, 6.0, ((0, 512),), jnp.float32),
        "eigvecs": bell_draw(key_of[5], (CENTRES, EIGEN), (CENTRES // 8) ** -0.5, 0.1875, ((0, 512),), jnp.float32),
        "eigscale": jnp.clip(jax.random.uniform(key_of[6], (EIGEN,), jnp.float32, 0.1, 0.95), 0.1, 0.95),
    }


def reference(pool, sample_index, targets, centres, coeffs, eigvecs, eigscale):
    highest = lax.Precision.HIGHEST
    owner = jnp.arange(ROWS, dtype=jnp.int32) // ROWS_DEV
    picks = (owner * SAMPLES_DEV + sample_index).astype(jnp.int32)
    batch_x = jnp.take(pool, picks, axis=0)
    inv_width = 1.0 / jnp.sqrt(jnp.float32(FEATURES))
    model_norm = 1.0 / jnp.sqrt(jnp.float32(CENTRES))
    blocks = N_BATCH
    block_rows = CENTRES // blocks
    zs = centres.reshape(blocks, block_rows, FEATURES)
    cs = coeffs.reshape(blocks, block_rows, OUTPUTS)

    def kernel_block(zblock):
        return jnp.exp(jnp.dot(batch_x, zblock.T, precision=highest, preferred_element_type=jnp.float32) * inv_width)

    def add_pred(totals, pieces):
        zblock, cblock = pieces
        return (totals + jnp.dot(kernel_block(zblock), cblock, precision=highest, preferred_element_type=jnp.float32), None)
    summed, unused = lax.scan(add_pred, jnp.zeros((ROWS, OUTPUTS), jnp.float32), (zs, cs))
    residual = summed * model_norm - targets

    def grad_block(zblock):
        return jnp.dot(kernel_block(zblock).T, residual, precision=highest, preferred_element_type=jnp.float32)
    gradient = lax.map(grad_block, zs).reshape(CENTRES, OUTPUTS) * model_norm
    coords = jnp.dot(eigvecs.T, gradient, precision=highest, preferred_element_type=jnp.float32)
    correction = jnp.dot(eigvecs, eigscale[:, None] * coords, precision=highest, preferred_element_type=jnp.float32)
    step_size = 0.5 * jnp.sqrt(jnp.float32(CENTRES) / jnp.float32(ROWS))
    return coeffs - step_size * (gradient - correction)
```

```python
import jax
import jax.numpy as jnp
from jax import lax
from jax.sharding import Mesh
from jax.sharding import PartitionSpec as P

PLANE = ("y", "x")
LINE = "z"
CORE = "core"
EVERY = ("y", "x", "z", "core")
HIGHEST = lax.Precision.HIGHEST


def product(left, right, left_dim, right_dim):
    return lax.dot_general(
        left,
        right,
        (((left_dim,), (right_dim,)), ((), ())),
        precision=HIGHEST,
        preferred_element_type=jnp.float32,
    )


def swapped(value):
    return lax.ppermute(value, CORE, [(0, 1), (1, 0)])


def exchanged(blocks, axis):
    return lax.all_to_all(blocks, axis, split_axis=0, concat_axis=0, tiled=True)


def to_all(value, axis):
    return exchanged(jnp.broadcast_to(value, (lax.axis_size(axis), *value.shape)), axis)


def on_device(pool, sample_index, targets, centres, coeffs, eigvecs, eigscale):
    n_plane = lax.axis_size(PLANE)
    n_line = lax.axis_size(LINE)
    n_core = lax.axis_size(CORE)
    own = centres.shape[0]
    rows = sample_index.shape[0]
    half = rows // n_core
    feats = pool.shape[1]
    width = centres.shape[1]
    outs = coeffs.shape[1]
    total_centres = own * n_plane * n_line * n_core
    total_rows = rows * n_plane
    core = lax.axis_index(CORE)

    merged = jnp.concatenate([centres, coeffs, eigvecs], axis=1)
    mine = to_all(merged, PLANE).reshape(own * n_plane, -1)
    other = swapped(mine)

    picked = jnp.take(pool, sample_index, axis=0).reshape(n_core, half, feats)
    keep = lax.dynamic_index_in_dim(picked, core, 0, keepdims=False)
    give = lax.dynamic_index_in_dim(picked, 1 - core, 0, keepdims=False)
    come = swapped(give)
    pair = jnp.where(core == 0, jnp.stack([keep, come]), jnp.stack([come, keep]))
    pair = pair.transpose(0, 2, 1).reshape(n_core * feats // 2, 2 * half)
    batch_t = to_all(pair, LINE).reshape(width, half)

    def kernel_of(z):
        return jnp.exp(product(batch_t, z, 0, 1) * (1.0 / jnp.sqrt(jnp.float32(width))))

    k_mine = kernel_of(mine[:, :width])
    k_other = kernel_of(other[:, :width])
    part = product(k_mine, mine[:, width:], 1, 0) + product(k_other, other[:, width:], 1, 0)
    part = exchanged(part.reshape(n_line, half // n_line, -1), LINE).sum(axis=0)
    whole = to_all(part, LINE).reshape(half, -1)

    model_norm = 1.0 / jnp.sqrt(jnp.float32(total_centres))
    own_targets = lax.dynamic_slice_in_dim(targets, core * half, half, 0)
    residual = whole[:, :outs] * model_norm - own_targets
    scaled = whole[:, outs:] * eigscale

    def change_of(k, v):
        return product(k - product(scaled, v, 1, 1), residual, 0, 0)

    change = change_of(k_mine, mine[:, width + outs :]) + swapped(
        change_of(k_other, other[:, width + outs :])
    )
    change = exchanged(change.reshape(n_plane, own, outs), PLANE).sum(axis=0)
    step_size = 0.5 * jnp.sqrt(jnp.float32(total_centres) / jnp.float32(total_rows))
    return coeffs - (step_size * model_norm) * change


def solution(mesh):
    finer = Mesh(mesh.devices.reshape(4, 4, 16, 2), EVERY)
    placed = (
        P(PLANE, (LINE, CORE)),
        P(PLANE),
        P(PLANE, None),
        P(EVERY, None),
        P(EVERY, None),
        P(EVERY, None),
        P(),
    )
    return jax.shard_map(
        on_device, mesh=finer, in_specs=placed, out_specs=P(EVERY, None), check_vma=False
    )
```

```python
import jax
import jax.numpy as jnp
from jax import lax
from jax.sharding import Mesh
from jax.sharding import PartitionSpec as P

PLANE = ("y", "x")
LINE = "z"
CORE = "core"
EVERY = ("y", "x", "z", "core")
HIGHEST = lax.Precision.HIGHEST


def product(left, right, left_dim, right_dim):
    return lax.dot_general(
        left,
        right,
        (((left_dim,), (right_dim,)), ((), ())),
        precision=HIGHEST,
        preferred_element_type=jnp.float32,
    )


def swapped(value):
    return lax.ppermute(value, CORE, [(0, 1), (1, 0)])


def exchanged(blocks, axis):
    return lax.all_to_all(blocks, axis, split_axis=0, concat_axis=0, tiled=True)


def to_all(value, axis):
    return exchanged(jnp.broadcast_to(value, (lax.axis_size(axis), *value.shape)), axis)


def on_device(pool, sample_index, targets, centres, coeffs, eigvecs, eigscale):
    n_plane = lax.axis_size(PLANE)
    n_line = lax.axis_size(LINE)
    n_core = lax.axis_size(CORE)
    own = centres.shape[0]
    rows = sample_index.shape[0]
    half = rows // n_core
    feats = pool.shape[1]
    width = centres.shape[1]
    outs = coeffs.shape[1]
    total_centres = own * n_plane * n_line * n_core
    total_rows = rows * n_plane
    core = lax.axis_index(CORE)

    merged = jnp.concatenate([centres, coeffs, eigvecs], axis=1)
    mine = to_all(merged, PLANE).reshape(own * n_plane, -1)

    picked = jnp.take(pool, sample_index, axis=0).reshape(n_core, half, feats)
    keep = lax.dynamic_index_in_dim(picked, core, 0, keepdims=False)
    give = lax.dynamic_index_in_dim(picked, 1 - core, 0, keepdims=False)
    come = swapped(give)
    pair = jnp.where(core == 0, jnp.stack([keep, come]), jnp.stack([come, keep]))
    pair = pair.transpose(0, 2, 1).reshape(n_core * feats // 2, 2 * half)
    batch_t = lax.all_gather(pair, LINE).reshape(width, half)

    mine, batch_t = lax.optimization_barrier((mine, batch_t))
    other = swapped(mine)

    def kernel_of(z):
        return jnp.exp(product(batch_t, z, 0, 1) * (1.0 / jnp.sqrt(jnp.float32(width))))

    k_mine = kernel_of(mine[:, :width])
    k_other = kernel_of(other[:, :width])
    part = product(k_mine, mine[:, width:], 1, 0) + product(k_other, other[:, width:], 1, 0)
    part = exchanged(part.reshape(n_line, half // n_line, -1), LINE).sum(axis=0)
    whole = to_all(part, LINE).reshape(half, -1)

    model_norm = 1.0 / jnp.sqrt(jnp.float32(total_centres))
    own_targets = lax.dynamic_slice_in_dim(targets, core * half, half, 0)
    residual = whole[:, :outs] * model_norm - own_targets
    scaled = whole[:, outs:] * eigscale

    def change_of(k, v):
        return product(k - product(scaled, v, 1, 1), residual, 0, 0)

    change = change_of(k_mine, mine[:, width + outs :]) + swapped(
        change_of(k_other, other[:, width + outs :])
    )
    change = exchanged(change.reshape(n_plane, own, outs), PLANE).sum(axis=0)
    step_size = 0.5 * jnp.sqrt(jnp.float32(total_centres) / jnp.float32(total_rows))
    return coeffs - (step_size * model_norm) * change


def solution(mesh):
    finer = Mesh(mesh.devices.reshape(4, 4, 16, 2), EVERY)
    placed = (
        P(PLANE, (LINE, CORE)),
        P(PLANE),
        P(PLANE, None),
        P(EVERY, None),
        P(EVERY, None),
        P(EVERY, None),
        P(),
    )
    return jax.shard_map(
        on_device, mesh=finer, in_specs=placed, out_specs=P(EVERY, None), check_vma=False
    )
```

```python
import jax
import jax.numpy as jnp
from jax import lax
from jax.sharding import Mesh
from jax.sharding import PartitionSpec as P

PLANE = ("y", "x")
LINE = "z"
CORE = "core"
CENTRE = ("z", "core")
EVERY = ("y", "x", "z", "core")


def product(left, right, left_dim, right_dim, precision=lax.Precision.HIGH):
    return lax.dot_general(
        left,
        right,
        (((left_dim,), (right_dim,)), ((), ())),
        precision=precision,
        preferred_element_type=jnp.float32,
    )


def swapped(value):
    return lax.ppermute(value, CORE, [(0, 1), (1, 0)])


def exchanged(blocks, axis):
    return lax.all_to_all(blocks, axis, split_axis=0, concat_axis=0, tiled=True)


def to_all(value, axis):
    return exchanged(jnp.broadcast_to(value, (lax.axis_size(axis), *value.shape)), axis)


def on_device(pool, sample_index, targets, centres, coeffs, eigvecs, eigscale):
    n_plane = lax.axis_size(PLANE)
    n_line = lax.axis_size(LINE)
    n_core = lax.axis_size(CORE)
    own, width = centres.shape
    rows = sample_index.shape[0]
    half = rows // n_core
    outs = coeffs.shape[1]
    total_centres = own * n_plane * n_line * n_core
    total_rows = rows * n_plane
    core = lax.axis_index(CORE)

    merged = jnp.concatenate([centres, coeffs, eigvecs], axis=1)
    group = to_all(merged, PLANE).reshape(own * n_plane, -1)

    chosen = lax.broadcasted_iota(jnp.int32, (pool.shape[0], rows), 0) == sample_index[None, :]
    picked = product(pool, chosen.astype(jnp.float32), 0, 0, lax.Precision.HIGHEST)
    batch_t = lax.all_gather(picked, CENTRE, axis=0, tiled=True)
    group, batch_t = lax.optimization_barrier((group, batch_t))

    zrows, terms = group[:, :width], group[:, width:]
    kernel = jnp.exp(product(batch_t, zrows, 0, 1) * (1.0 / jnp.sqrt(jnp.float32(width))))

    give = product(lax.dynamic_slice_in_dim(kernel, (1 - core) * half, half, 0), terms, 1, 0)
    come = swapped(give)
    part = product(lax.dynamic_slice_in_dim(kernel, core * half, half, 0), terms, 1, 0) + come
    tall, wide = 8, part.shape[1] * half // 8 // n_line
    across = part.shape[1] // wide
    blocks = part.reshape(half // tall, tall, across, wide).transpose(0, 2, 1, 3)
    own_sum = exchanged(blocks.reshape(n_line, tall, wide), LINE).sum(axis=0)
    whole = lax.all_gather(own_sum, CENTRE, axis=0)
    whole = whole.reshape(half // tall, across, n_core, tall, wide).transpose(2, 0, 3, 1, 4)
    whole = whole.reshape(rows, -1)

    model_norm = 1.0 / jnp.sqrt(jnp.float32(total_centres))
    residual = whole[:, :outs] * model_norm - targets
    scaled = whole[:, outs:] * eigscale
    weight = kernel - product(scaled, terms[:, outs:], 1, 1)
    change = product(weight, residual, 0, 0)
    change = exchanged(change.reshape(n_plane, own, outs), PLANE).sum(axis=0)
    step_size = 0.5 * jnp.sqrt(jnp.float32(total_centres) / jnp.float32(total_rows))
    return coeffs - (step_size * model_norm) * change


def solution(mesh):
    finer = Mesh(mesh.devices.reshape(4, 4, 16, 2), EVERY)
    placed = (
        P(PLANE, CENTRE),
        P(PLANE),
        P(PLANE, None),
        P(EVERY, None),
        P(EVERY, None),
        P(EVERY, None),
        P(),
    )
    return jax.shard_map(
        on_device, mesh=finer, in_specs=placed, out_specs=P(EVERY, None), check_vma=False
    )
```

```python
import jax
import jax.numpy as jnp
from jax import lax
from jax.sharding import Mesh
from jax.sharding import PartitionSpec as P

PLANE = ("y", "x")
FAR = "z_far"
NEAR = "z_near"
CORE = "core"
NEAR_CORE = ("z_near", "core")
CENTRE = ("z_far", "z_near", "core")
EVERY = ("y", "x", "z_far", "z_near", "core")


def product(left, right, left_dim, right_dim, precision=lax.Precision.HIGH):
    return lax.dot_general(
        left,
        right,
        (((left_dim,), (right_dim,)), ((), ())),
        precision=precision,
        preferred_element_type=jnp.float32,
    )


def swapped(value):
    return lax.ppermute(value, CORE, [(0, 1), (1, 0)])


def exchanged(blocks, axis):
    return lax.all_to_all(blocks, axis, split_axis=0, concat_axis=0, tiled=True)


def to_all(value, axis):
    return exchanged(jnp.broadcast_to(value, (lax.axis_size(axis), *value.shape)), axis)


def on_device(pool, sample_index, targets, centres, coeffs, eigvecs, eigscale):
    n_plane = lax.axis_size(PLANE)
    n_near = lax.axis_size(NEAR)
    n_core = lax.axis_size(CORE)
    own, width = centres.shape
    rows = sample_index.shape[0]
    outs = coeffs.shape[1]
    total_centres = own * n_plane * lax.axis_size(CENTRE)
    total_rows = rows * n_plane
    core = lax.axis_index(CORE)

    merged = jnp.concatenate([centres, coeffs, eigvecs], axis=1)
    group = to_all(merged, PLANE).reshape(own * n_plane, -1)

    chosen = lax.broadcasted_iota(jnp.int32, (pool.shape[0], rows), 0) == sample_index[None, :]
    picked = product(pool, chosen.astype(jnp.float32), 0, 0, lax.Precision.HIGHEST)
    batch_t = lax.all_gather(picked, CENTRE, axis=0, tiled=True)
    group, batch_t = lax.optimization_barrier((group, batch_t))

    zrows, terms = group[:, :width], group[:, width:]
    kernel = jnp.exp(product(batch_t, zrows, 0, 1) * (1.0 / jnp.sqrt(jnp.float32(width))))

    tall = rows // (n_near * n_core)
    by_core = kernel.reshape(n_near, n_core, tall, -1)

    def term_sums(of_core):
        taken = lax.dynamic_index_in_dim(by_core, of_core, 1, keepdims=False)
        return product(taken.reshape(rows // n_core, -1), terms, 1, 0)

    part = swapped(term_sums(1 - core)) + term_sums(core)
    near_sum = exchanged(part.reshape(n_near, tall, -1), NEAR).sum(axis=0)
    own_sum = lax.all_gather(near_sum, FAR, axis=0).sum(axis=0)
    whole = lax.all_gather(own_sum, NEAR_CORE, axis=0, tiled=True)

    model_norm = 1.0 / jnp.sqrt(jnp.float32(total_centres))
    residual = whole[:, :outs] * model_norm - targets
    scaled = whole[:, outs:] * eigscale
    weight = kernel - product(scaled, terms[:, outs:], 1, 1)
    change = product(weight, residual, 0, 0)
    change = exchanged(change.reshape(n_plane, own, outs), PLANE).sum(axis=0)
    step_size = 0.5 * jnp.sqrt(jnp.float32(total_centres) / jnp.float32(total_rows))
    return coeffs - (step_size * model_norm) * change


def solution(mesh):
    finer = Mesh(mesh.devices.reshape(4, 4, 4, 4, 2), EVERY)
    placed = (
        P(PLANE, CENTRE),
        P(PLANE),
        P(PLANE, None),
        P(EVERY, None),
        P(EVERY, None),
        P(EVERY, None),
        P(),
    )
    return jax.shard_map(
        on_device, mesh=finer, in_specs=placed, out_specs=P(EVERY, None), check_vma=False
    )
```

```python
import jax
import jax.numpy as jnp
from jax import lax
from jax.sharding import Mesh
from jax.sharding import PartitionSpec as P

PLANE = "plane"
ORDER = [[2, 12, 0, 14, 1, 5, 3, 7, 10, 4, 8, 6, 9, 13, 11, 15]]
FAR = "z_far"
NEAR = "z_near"
CORE = "core"
NEAR_CORE = ("z_near", "core")
CENTRE = ("z_far", "z_near", "core")
EVERY = ("plane", "z_far", "z_near", "core")


def product(left, right, left_dim, right_dim, precision=lax.Precision.HIGH):
    return lax.dot_general(
        left,
        right,
        (((left_dim,), (right_dim,)), ((), ())),
        precision=precision,
        preferred_element_type=jnp.float32,
    )


def swapped(value):
    return lax.ppermute(value, CORE, [(0, 1), (1, 0)])


def exchanged(blocks, axis, groups=None):
    return lax.all_to_all(
        blocks, axis, split_axis=0, concat_axis=0, axis_index_groups=groups, tiled=True
    )


def to_all(value, axis, groups=None):
    return exchanged(jnp.broadcast_to(value, (lax.axis_size(axis), *value.shape)), axis, groups)


def on_device(pool, sample_index, targets, centres, coeffs, eigvecs, eigscale):
    n_plane = lax.axis_size(PLANE)
    n_near = lax.axis_size(NEAR)
    n_core = lax.axis_size(CORE)
    own, width = centres.shape
    rows = sample_index.shape[0]
    outs = coeffs.shape[1]
    total_centres = own * n_plane * lax.axis_size(CENTRE)
    total_rows = rows * n_plane
    core = lax.axis_index(CORE)

    merged = jnp.concatenate([centres, coeffs, eigvecs], axis=1)
    group = to_all(merged, PLANE, ORDER).reshape(own * n_plane, -1)

    chosen = lax.broadcasted_iota(jnp.int32, (pool.shape[0], rows), 0) == sample_index[None, :]
    picked = product(pool, chosen.astype(jnp.float32), 0, 0, lax.Precision.HIGHEST)
    batch_t = lax.all_gather(picked, CENTRE, axis=0, tiled=True)
    group, batch_t = lax.optimization_barrier((group, batch_t))

    zrows, terms = group[:, :width], group[:, width:]
    kernel = jnp.exp(product(batch_t, zrows, 0, 1) * (1.0 / jnp.sqrt(jnp.float32(width))))

    tall = rows // (n_near * n_core)
    by_core = kernel.reshape(n_near, n_core, tall, -1)

    def term_sums(of_core):
        taken = lax.dynamic_index_in_dim(by_core, of_core, 1, keepdims=False)
        return product(taken.reshape(rows // n_core, -1), terms, 1, 0)

    part = swapped(term_sums(1 - core)) + term_sums(core)
    near_sum = exchanged(part.reshape(n_near, tall, -1), NEAR).sum(axis=0)
    own_sum = lax.all_gather(near_sum, FAR, axis=0).sum(axis=0)
    whole = lax.all_gather(own_sum, NEAR_CORE, axis=0, tiled=True)

    model_norm = 1.0 / jnp.sqrt(jnp.float32(total_centres))
    residual = whole[:, :outs] * model_norm - targets
    scaled = whole[:, outs:] * eigscale
    weight = kernel - product(scaled, terms[:, outs:], 1, 1)
    change = product(weight, residual, 0, 0)
    change = exchanged(change.reshape(n_plane, own, outs), PLANE, ORDER).sum(axis=0)
    step_size = 0.5 * jnp.sqrt(jnp.float32(total_centres) / jnp.float32(total_rows))
    return coeffs - (step_size * model_norm) * change


def solution(mesh):
    finer = Mesh(mesh.devices.reshape(16, 4, 4, 2), EVERY)
    placed = (
        P(PLANE, CENTRE),
        P(PLANE),
        P(PLANE, None),
        P(EVERY, None),
        P(EVERY, None),
        P(EVERY, None),
        P(),
    )
    return jax.shard_map(
        on_device, mesh=finer, in_specs=placed, out_specs=P(EVERY, None), check_vma=False
    )
```

```python
import jax
import jax.numpy as jnp
from jax import lax
from jax.sharding import Mesh
from jax.sharding import PartitionSpec as P

PLANE = "plane"
ORDER = [[2, 12, 0, 14, 1, 5, 3, 7, 10, 4, 8, 6, 9, 13, 11, 15]]
FAR = "z_far"
NEAR = "z_near"
CORE = "core"
NEAR_CORE = ("z_near", "core")
CENTRE = ("z_far", "z_near", "core")
NEAR_ORDER = [[0, 1, 3, 2]]
NEAR_CORE_ORDER = [[2 * near + core for near in NEAR_ORDER[0] for core in range(2)]]
EVERY = ("plane", "z_far", "z_near", "core")


def product(left, right, left_dim, right_dim, precision=lax.Precision.HIGH):
    return lax.dot_general(
        left,
        right,
        (((left_dim,), (right_dim,)), ((), ())),
        precision=precision,
        preferred_element_type=jnp.float32,
    )


def swapped(value):
    return lax.ppermute(value, CORE, [(0, 1), (1, 0)])


def exchanged(blocks, axis, groups=None):
    return lax.all_to_all(
        blocks, axis, split_axis=0, concat_axis=0, axis_index_groups=groups, tiled=True
    )


def to_all(value, axis, groups=None):
    return exchanged(jnp.broadcast_to(value, (lax.axis_size(axis), *value.shape)), axis, groups)


def on_device(pool, sample_index, targets, centres, coeffs, eigvecs, eigscale):
    n_plane = lax.axis_size(PLANE)
    n_near = lax.axis_size(NEAR)
    n_core = lax.axis_size(CORE)
    own, width = centres.shape
    rows = sample_index.shape[0]
    outs = coeffs.shape[1]
    total_centres = own * n_plane * lax.axis_size(CENTRE)
    total_rows = rows * n_plane
    core = lax.axis_index(CORE)

    merged = jnp.concatenate([centres, coeffs, eigvecs], axis=1)
    group = to_all(merged, PLANE, ORDER).reshape(own * n_plane, -1)

    chosen = lax.broadcasted_iota(jnp.int32, (pool.shape[0], rows), 0) == sample_index[None, :]
    picked = product(pool, chosen.astype(jnp.float32), 0, 0, lax.Precision.HIGHEST)
    batch_t = lax.all_gather(picked, CENTRE, axis=0, tiled=True)
    group, batch_t = lax.optimization_barrier((group, batch_t))

    zrows, terms = group[:, :width], group[:, width:]
    kernel = jnp.exp(product(batch_t, zrows, 0, 1) * (1.0 / jnp.sqrt(jnp.float32(width))))

    tall = rows // (n_near * n_core)
    by_core = kernel.reshape(n_near, n_core, tall, -1)

    def term_sums(of_core):
        taken = lax.dynamic_index_in_dim(by_core, of_core, 1, keepdims=False)
        return product(taken.reshape(rows // n_core, -1), terms, 1, 0)

    part = swapped(term_sums(1 - core)) + term_sums(core)
    near_sum = exchanged(part.reshape(n_near, tall, -1), NEAR, NEAR_ORDER).sum(axis=0)
    own_sum = lax.all_gather(near_sum, FAR, axis=0).sum(axis=0)
    whole = lax.all_gather(
        own_sum, NEAR_CORE, axis_index_groups=NEAR_CORE_ORDER, axis=0, tiled=True
    )

    model_norm = 1.0 / jnp.sqrt(jnp.float32(total_centres))
    residual = whole[:, :outs] * model_norm - targets
    scaled = whole[:, outs:] * eigscale
    weight = kernel - product(scaled, terms[:, outs:], 1, 1)
    change = product(weight, residual, 0, 0)
    change = exchanged(change.reshape(n_plane, own, outs), PLANE, ORDER).sum(axis=0)
    step_size = 0.5 * jnp.sqrt(jnp.float32(total_centres) / jnp.float32(total_rows))
    return coeffs - (step_size * model_norm) * change


def solution(mesh):
    finer = Mesh(mesh.devices.reshape(16, 4, 4, 2), EVERY)
    placed = (
        P(PLANE, CENTRE),
        P(PLANE),
        P(PLANE, None),
        P(EVERY, None),
        P(EVERY, None),
        P(EVERY, None),
        P(),
    )
    return jax.shard_map(
        on_device, mesh=finer, in_specs=placed, out_specs=P(EVERY, None), check_vma=False
    )
```

```python
import jax
import jax.numpy as jnp
from jax import lax
from jax.sharding import Mesh
from jax.sharding import PartitionSpec as P

PLANE = "plane"
ORDER = [[2, 12, 0, 14, 1, 5, 3, 7, 10, 4, 8, 6, 9, 13, 11, 15]]
FAR = "z_far"
NEAR = "z_near"
CORE = "core"
NEAR_CORE = ("z_near", "core")
CENTRE = ("z_far", "z_near", "core")
NEAR_ORDER = [[0, 1, 3, 2]]
NEAR_CORE_ORDER = [[2 * near + core for near in NEAR_ORDER[0] for core in range(2)]]
EVERY = ("plane", "z_far", "z_near", "core")


def product(left, right, left_dim, right_dim, precision=lax.Precision.HIGH):
    return lax.dot_general(
        left,
        right,
        (((left_dim,), (right_dim,)), ((), ())),
        precision=precision,
        preferred_element_type=jnp.float32,
    )


def swapped(value):
    return lax.ppermute(value, CORE, [(0, 1), (1, 0)])


def exchanged(blocks, axis, groups=None):
    return lax.all_to_all(
        blocks, axis, split_axis=0, concat_axis=0, axis_index_groups=groups, tiled=True
    )


def to_all(value, axis, groups=None):
    return exchanged(jnp.broadcast_to(value, (lax.axis_size(axis), *value.shape)), axis, groups)


def on_device(pool, sample_index, targets, centres, coeffs, eigvecs, eigscale):
    n_plane = lax.axis_size(PLANE)
    n_near = lax.axis_size(NEAR)
    n_core = lax.axis_size(CORE)
    own, width = centres.shape
    rows = sample_index.shape[0]
    outs = coeffs.shape[1]
    total_centres = own * n_plane * lax.axis_size(CENTRE)
    total_rows = rows * n_plane
    core = lax.axis_index(CORE)

    merged = jnp.concatenate([centres, coeffs, eigvecs], axis=1)
    group = to_all(merged, PLANE, ORDER).reshape(own * n_plane, -1)

    chosen = lax.broadcasted_iota(jnp.int32, (pool.shape[0], rows), 0) == sample_index[None, :]
    picked = product(pool, chosen.astype(jnp.float32), 0, 0, lax.Precision.HIGHEST)
    batch_t = lax.all_gather(picked, CENTRE, axis=0, tiled=True)
    group, batch_t = lax.optimization_barrier((group, batch_t))

    zrows, terms = group[:, :width], group[:, width:]
    kernel = jnp.exp(product(batch_t, zrows, 0, 1) * (1.0 / jnp.sqrt(jnp.float32(width))))

    tall = rows // (n_near * n_core)
    by_core = kernel.reshape(n_near, n_core, tall, -1)

    def term_sums(by_core, of_core):
        taken = lax.dynamic_index_in_dim(by_core, of_core, 1, keepdims=False)
        return product(taken.reshape(rows // n_core, -1), terms, 1, 0)

    give, kept_rows = lax.optimization_barrier((term_sums(by_core, 1 - core), by_core))
    come, keep = lax.optimization_barrier((swapped(give), term_sums(kept_rows, core)))
    part = come + keep
    near_sum = exchanged(part.reshape(n_near, tall, -1), NEAR, NEAR_ORDER).sum(axis=0)
    own_sum = lax.all_gather(near_sum, FAR, axis=0).sum(axis=0)
    whole = lax.all_gather(
        own_sum, NEAR_CORE, axis_index_groups=NEAR_CORE_ORDER, axis=0, tiled=True
    )

    model_norm = 1.0 / jnp.sqrt(jnp.float32(total_centres))
    residual = whole[:, :outs] * model_norm - targets
    scaled = whole[:, outs:] * eigscale
    weight = kernel - product(scaled, terms[:, outs:], 1, 1)
    change = product(weight, residual, 0, 0)
    change = exchanged(change.reshape(n_plane, own, outs), PLANE, ORDER).sum(axis=0)
    step_size = 0.5 * jnp.sqrt(jnp.float32(total_centres) / jnp.float32(total_rows))
    return coeffs - (step_size * model_norm) * change


def solution(mesh):
    finer = Mesh(mesh.devices.reshape(16, 4, 4, 2), EVERY)
    placed = (
        P(PLANE, CENTRE),
        P(PLANE),
        P(PLANE, None),
        P(EVERY, None),
        P(EVERY, None),
        P(EVERY, None),
        P(),
    )
    return jax.shard_map(
        on_device, mesh=finer, in_specs=placed, out_specs=P(EVERY, None), check_vma=False
    )
```
